32 devices in a mesh: gx: 16 (over z, y, x), gy: 2 (over core).
Axes of the slice: x: 2, y: 2, z: 4, core: 2. Of those that a mesh axis runs over, the one named last changes fastest.
Arguments:
- blocks_a: bfloat16 [16, 16, 5, 4096], P('gx', 'gy'), may hold values from -0.75 to 0.75
- prolong: bfloat16 [16, 16, 4096], P('gx', 'gy'), may hold values from -1.5 to 1.5
- aggregate: int32 [16, 16], P('gx', 'gy'), may hold values from 0 to 15, as said below
- coupling_slot: int32 [16, 16, 5], P('gx', 'gy'), may hold values from 0 to 7
Outputs:
- coarse: float32 [16, 2, 8, 4096], P('gx', 'gy')
The draws below stay inside these ranges and needn't reach their ends.
Inputs may be any that keep to these rules, and one draw needn't show every extreme that they name: The aggregate a of an element is held by the device of gx index a // 1 in the element's own gy column. Of the elements of any one device at most 2 have aggregates held by one gx index, and on every device some gx index holds exactly 2 of them.
All inputs are finite; a program needn't handle non-finite values.
Results may differ from the reference program's by a relative error of at most 0.004.
Values may be sent and summed in bfloat16 or wider, within the bound.
A program may use at most 64 MiB of HBM per device.

```python
import jax
import jax.numpy as jnp
from jax import lax

B = 64
K = 5
CS = 8
CX = 1
CY = 8
AGG_DEV = 1
CAP = 2
NX = 16
NY = 16
AGGS = 16
N_GX = 16
N_GY = 2


def draw_aggregate(key, part):
    devices = N_GX * N_GY
    per_device = CX * CY
    eligible_clusters = N_GX * CAP
    prospective_cluster = (jnp.arange(eligible_clusters, dtype=jnp.int32) // CAP).astype(jnp.int32)
    base = jax.random.fold_in(key, 7001)

    def one_device(index):
        subkey = jax.random.fold_in(base, index)
        keys = jax.random.split(subkey, 5)
        likeliest_cluster = jax.random.randint(keys[0], (), 0, N_GX)
        inclination_factor = jax.random.randint(keys[1], (N_GX,), 0, 4)
        stochastic_perturbation = jax.random.randint(keys[2], (eligible_clusters,), 0, 65536)
        kinship_increment = (prospective_cluster == likeliest_cluster).astype(jnp.int32) * 262144
        selection_merit = (stochastic_perturbation + inclination_factor[prospective_cluster] * 65536 + kinship_increment) * eligible_clusters + jnp.arange(eligible_clusters, dtype=jnp.int32)
        chosen = lax.top_k(selection_merit, per_device)[1]
        owners = jax.random.permutation(keys[3], prospective_cluster[chosen])
        local_id = jax.random.randint(keys[4], (per_device,), 0, AGG_DEV)
        return owners * AGG_DEV + local_id
    table = jax.vmap(one_device)(jnp.arange(devices, dtype=jnp.int32))
    return table.reshape(N_GX, N_GY, CX, CY).transpose(0, 2, 1, 3).reshape(N_GX * CX, N_GY * CY).astype(jnp.int32)


def with_ends(array, own_key, low, largest):
    extent = array.shape
    place = [jax.random.randint(jax.random.fold_in(own_key, axis), (), 0, extent[axis]) for axis in range(len(extent))]
    array = array.at[tuple(place)].set(low)
    longest = extent.index(max(extent))
    place[longest] = (place[longest] + 1) % extent[longest]
    return array.at[tuple(place)].set(largest)


def levels(own_key, extent, cuts, least, largest):
    loudness, own = 1.0, jax.random.fold_in(own_key, 6)
    for dim, blocks in cuts:
        steps = jnp.exp(jax.random.uniform(jax.random.fold_in(own, dim), (blocks,), jnp.float32, least / len(cuts), largest / len(cuts)))
        loudness = loudness * jnp.repeat(steps, extent[dim] // blocks).reshape([-1 if axis == dim else 1 for axis in range(len(extent))])
    return loudness


def gaussian(own_key, extent, deviation, reach, cuts=(), kind=jnp.bfloat16):
    loudness = levels(own_key, extent, cuts, -0.22, 0.18) if cuts else 1.0
    entries = jax.random.normal(own_key, extent, jnp.float32) * deviation * loudness
    return jnp.minimum(jnp.maximum(entries, -reach), reach).astype(kind)


def setup_inputs(seed: int = 0) -> dict:
    key_of = jax.random.split(jax.random.key(seed), 5)
    blocks_a = gaussian(key_of[0], (NX, NY, K, B * B), B ** -0.5, 0.75, ((0, 16), (1, 2)))
    prolong = gaussian(key_of[1], (NX, NY, B * B), 0.25, 1.5, ((0, 16), (1, 2)))
    aggregate = draw_aggregate(jax.random.fold_in(key_of[4], 71), 0)
    coupling_slot = with_ends(jax.random.randint(key_of[3], (NX, NY, K), 0, CS), jax.random.fold_in(key_of[3], 1), 0, CS - 1).astype(jnp.int32)
    return {"blocks_a": blocks_a, "prolong": prolong, "aggregate": aggregate, "coupling_slot": coupling_slot}


def reference(blocks_a, prolong, aggregate, coupling_slot):
    block_len = B * B
    padded = jnp.pad(prolong, ((1, 1), (1, 1), (0, 0)))
    column_of = (jnp.arange(NY, dtype=jnp.int32) // CY).astype(jnp.int32)

    def row_step(coarse_flat, index):
        a_row = lax.dynamic_index_in_dim(blocks_a, index, 0, keepdims=False)
        window = lax.dynamic_slice_in_dim(padded, index, 3, 0)
        beside = jnp.stack([window[1, 1:-1], window[0, 1:-1], window[2, 1:-1], window[1, :-2], window[1, 2:]], axis=1)
        matrix_a = a_row.reshape(NY, K, B, B).astype(jnp.float32)
        matrix_p = beside.reshape(NY, K, B, B).astype(jnp.float32)
        product = jnp.einsum("jkab,jkbc->jkac", matrix_a, matrix_p, precision=lax.Precision.HIGHEST).astype(jnp.bfloat16)
        product = lax.optimization_barrier(product).astype(jnp.float32)
        own_block = window[1, 1:-1].reshape(NY, B, B).astype(jnp.float32)
        contribution = jnp.einsum("jba,jkbc->jkac", own_block, product, precision=lax.Precision.HIGHEST).astype(jnp.bfloat16)
        contribution = lax.optimization_barrier(contribution).astype(jnp.float32)
        agg_row = lax.dynamic_index_in_dim(aggregate, index, 0, keepdims=False).astype(jnp.int32)
        slot_row = lax.dynamic_index_in_dim(coupling_slot, index, 0, keepdims=False).astype(jnp.int32)
        target = ((agg_row * N_GY + column_of)[:, None] * CS + slot_row).astype(jnp.int32)
        coarse_flat = coarse_flat.at[target.reshape(-1)].add(contribution.reshape(NY * K, block_len))
        return coarse_flat, None

    start = jnp.zeros((AGGS * N_GY * CS, block_len), jnp.float32)
    coarse_flat, unused = lax.scan(row_step, start, jnp.arange(NX, dtype=jnp.int32))
    return coarse_flat.reshape(AGGS, N_GY, CS, block_len)
```

```python
import functools

import jax
import jax.numpy as jnp
from jax import lax
from jax.experimental import pallas as pl
from jax.experimental.pallas import tpu as pltpu
from jax.sharding import PartitionSpec as P

B = 64
K = 5
CS = 8
MESH = pl.DeviceIdType.MESH


def neighbours(block, axis, dim):
    count = lax.axis_size(axis)
    forward = [(i, i + 1) for i in range(count - 1)]
    backward = [(target, source) for source, target in forward]
    last = lax.slice_in_dim(block, block.shape[dim] - 1, None, axis=dim)
    first = lax.slice_in_dim(block, 0, 1, axis=dim)
    low = lax.ppermute(last, axis, forward)
    high = lax.ppermute(first, axis, backward)
    return low, high


def bit_orders(n):
    bits = [1 << i for i in range(n.bit_length() - 1)]
    swapped = list(bits)
    for i in range(0, len(bits) - 1, 2):
        swapped[i], swapped[i + 1] = bits[i + 1], bits[i]
    return bits, swapped


def places(order):
    offsets = [0]
    for bit in reversed(order):
        offsets = offsets + [o | bit for o in offsets]
    return offsets


def exchange(n, orders, select_ref, rows_ref, out_ref, acc, *rest):
    steps = len(orders[0])
    send, recv = rest[:steps], rest[steps : 2 * steps]
    send_sem, recv_sem = rest[2 * steps :]
    me = lax.axis_index("gx")

    def partner(bit):
        return me + bit - 2 * bit * ((me // bit) % 2)

    barrier = pltpu.get_barrier_semaphore()
    for bit in orders[0]:
        pl.semaphore_signal(
            barrier, inc=1, device_id={"gx": partner(bit)}, device_id_type=MESH
        )

    width = rows_ref.shape[1] // 4

    def gathered(chain, low, high):
        select = select_ref[chain, low * CS : high * CS, :]
        parts = []
        for q in range(2):
            begin = (chain * 2 + q) * width
            part = jnp.dot(
                select, rows_ref[:, begin : begin + width], preferred_element_type=jnp.float32
            )
            parts.append(part.reshape(high - low, CS, width))
        return jnp.concatenate(parts, axis=1)

    def copy(chain, step):
        return pltpu.make_async_remote_copy(
            src_ref=send[step].at[chain],
            dst_ref=recv[step].at[chain],
            send_sem=send_sem.at[chain, step],
            recv_sem=recv_sem.at[chain, step],
            device_id={"gx": partner(orders[chain][step])},
            device_id_type=MESH,
        )

    half = n // 2
    for chain in range(2):
        send[0][chain] = gathered(chain, half, n).astype(jnp.bfloat16)
        if chain == 0:
            pl.semaphore_wait(barrier, steps)
        copy(chain, 0).start()
    for chain in range(2):
        acc[chain] = gathered(chain, 0, half)
    for step in range(steps):
        count = half >> step
        for chain in range(2):
            copy(chain, step).wait_recv()
            if step + 1 < steps:
                keep = count // 2
                send[step + 1][chain] = (
                    acc[chain, keep:count] + recv[step][chain, keep:count].astype(jnp.float32)
                ).astype(jnp.bfloat16)
                copy(chain, step + 1).start()
                acc[chain, 0:keep] = acc[chain, 0:keep] + recv[step][chain, 0:keep].astype(
                    jnp.float32
                )
            else:
                total = acc[chain, 0] + recv[step][chain, 0].astype(jnp.float32)
                for q in range(2):
                    begin = (chain * 2 + q) * width
                    out_ref[:, begin : begin + width] = total[q * CS : (q + 1) * CS, :]
    for step in range(steps):
        for chain in range(2):
            copy(chain, step).wait_send()


def body(blocks_a, prolong, aggregate, coupling_slot):
    grid_rows, grid_cols, block_len = prolong.shape
    elements = grid_rows * grid_cols
    n = lax.axis_size("gx")
    low_x, high_x = neighbours(prolong, "gx", 0)
    low_y, high_y = neighbours(prolong, "gy", 1)
    beside = jnp.stack(
        [
            prolong,
            jnp.concatenate([low_x, prolong[:-1]], axis=0),
            jnp.concatenate([prolong[1:], high_x], axis=0),
            jnp.concatenate([low_y, prolong[:, :-1]], axis=1),
            jnp.concatenate([prolong[:, 1:], high_y], axis=1),
        ],
        axis=2,
    )
    matrix_a = blocks_a.reshape(elements, K, B, B)
    matrix_p = beside.reshape(elements, K, B, B)
    product = jnp.einsum(
        "ekab,ekbc->ekac", matrix_a, matrix_p, preferred_element_type=jnp.float32
    ).astype(jnp.bfloat16)
    own_block = prolong.reshape(elements, B, B)
    contribution = jnp.einsum(
        "eba,ekbc->ekac", own_block, product, preferred_element_type=jnp.float32
    ).astype(jnp.bfloat16)
    rows = contribution.reshape(elements * K, block_len)

    orders = bit_orders(n)
    steps = len(orders[0])
    me = lax.axis_index("gx")
    offsets = jnp.asarray([places(order) for order in orders], jnp.int32)
    owner_at = jnp.bitwise_xor(offsets, me)
    wanted = owner_at[:, :, None] * CS + jnp.arange(CS, dtype=jnp.int32)[None, None, :]
    target = (aggregate.reshape(elements, 1) * CS + coupling_slot.reshape(elements, K)).reshape(-1)
    select = (wanted.reshape(2, n * CS, 1) == target[None, None, :]).astype(jnp.bfloat16)

    width = block_len // 4
    slots = [(2, n >> (step + 1), 2 * CS, width) for step in range(steps)]
    vmem = pl.BlockSpec(memory_space=pltpu.VMEM)
    coarse = pl.pallas_call(
        functools.partial(exchange, n, orders),
        out_shape=jax.ShapeDtypeStruct((CS, block_len), jnp.float32),
        in_specs=[vmem, vmem],
        out_specs=vmem,
        scratch_shapes=[pltpu.VMEM(slots[0], jnp.float32)]
        + [pltpu.VMEM(shape, jnp.bfloat16) for shape in slots + slots]
        + [pltpu.SemaphoreType.DMA((2, steps)), pltpu.SemaphoreType.DMA((2, steps))],
        compiler_params=pltpu.CompilerParams(
            collective_id=0, has_side_effects=True, vmem_limit_bytes=40 * 1024 * 1024
        ),
    )(select, rows)
    return coarse.reshape(1, 1, CS, block_len)


def solution(mesh):
    return jax.shard_map(
        body,
        mesh=mesh,
        in_specs=(
            P("gx", "gy", None, None),
            P("gx", "gy", None),
            P("gx", "gy"),
            P("gx", "gy", None),
        ),
        out_specs=P("gx", "gy", None, None),
        check_vma=False,
    )
```

```python
import functools

import jax
import jax.numpy as jnp
from jax import lax
from jax.experimental import pallas as pl
from jax.experimental.pallas import tpu as pltpu
from jax.sharding import PartitionSpec as P

B = 64
K = 5
CS = 8
MESH = pl.DeviceIdType.MESH


def bit_orders(n):
    bits = [1 << i for i in range(n.bit_length() - 1)]
    swapped = list(bits)
    for i in range(0, len(bits) - 1, 2):
        swapped[i], swapped[i + 1] = bits[i + 1], bits[i]
    return bits, swapped


def places(order):
    offsets = [0]
    for bit in reversed(order):
        offsets = offsets + [o | bit for o in offsets]
    return offsets


def coarsen(
    n, ny, orders, owner_ref, slot_ref, a_ref, p_ref, out_ref,
    low_x, high_x, low_y, high_y, sums, parts, acc, *rest,
):
    steps = len(orders[0])
    send, recv = rest[:steps], rest[steps : 2 * steps]
    send_sem, recv_sem, halo_send, halo_recv = rest[2 * steps :]
    me, column = lax.axis_index("gx"), lax.axis_index("gy")
    elements = p_ref.shape[0]

    def partner(bit):
        return me + bit - 2 * bit * ((me // bit) % 2)

    sides = [
        (me < n - 1, me > 0, {"gx": jnp.minimum(me + 1, n - 1)}, p_ref, low_x),
        (me > 0, me < n - 1, {"gx": jnp.maximum(me - 1, 0)}, p_ref, high_x),
        (column < ny - 1, column > 0, {"gy": jnp.minimum(column + 1, ny - 1)},
         p_ref.at[elements - 1], low_y),
        (column > 0, column < ny - 1, {"gy": jnp.maximum(column - 1, 0)}, p_ref.at[0], high_y),
    ]

    def halo(i):
        return pltpu.make_async_remote_copy(
            src_ref=sides[i][3], dst_ref=sides[i][4],
            send_sem=halo_send.at[i], recv_sem=halo_recv.at[i],
            device_id=sides[i][2], device_id_type=MESH,
        )

    barrier = pltpu.get_barrier_semaphore()
    for bit in orders[0]:
        pl.semaphore_signal(
            barrier, inc=1, device_id={"gx": partner(bit)}, device_id_type=MESH
        )
    for sends, _, target, _, _ in sides:
        @pl.when(sends)
        def _():
            pl.semaphore_signal(barrier, inc=1, device_id=target, device_id_type=MESH)
    expected = steps
    for sends, _, _, _, _ in sides:
        expected = expected + jnp.where(sends, 1, 0)
    pl.semaphore_wait(barrier, expected)
    for i, (sends, receives, _, _, place) in enumerate(sides):
        @pl.when(sends)
        def _():
            halo(i).start()

        @pl.when(jnp.logical_not(receives))
        def _():
            place[...] = jnp.zeros_like(place)
    for i in range(4):
        @pl.when(sides[i][1])
        def _():
            halo(i).wait_recv()

    for e in range(elements):
        beside = [
            p_ref[e], low_x[e], high_x[e],
            p_ref[e - 1] if e else low_y[...],
            p_ref[e + 1] if e + 1 < elements else high_y[...],
        ]
        products = [
            jnp.dot(a_ref[e * K + k], beside[k], preferred_element_type=jnp.float32)
            .astype(jnp.bfloat16).astype(jnp.float32)
            for k in range(K)
        ]
        for s in range(CS):
            total = products[0] * slot_ref[(e * K) * CS + s]
            for k in range(1, K):
                total = total + products[k] * slot_ref[(e * K + k) * CS + s]
            sums[e % 2, :, s * B : (s + 1) * B] = total.astype(jnp.bfloat16)
        parts[e] = (
            lax.dot_general(
                p_ref[e], sums[e % 2], (((0,), (0,)), ((), ())),
                preferred_element_type=jnp.float32,
            ).astype(jnp.bfloat16).astype(jnp.float32)
        )

    rows = B // 2

    def gathered(chain, place):
        base = (chain * n + place) * elements
        total = parts[0, chain * rows : (chain + 1) * rows, :] * owner_ref[base]
        for e in range(1, elements):
            total = total + parts[e, chain * rows : (chain + 1) * rows, :] * owner_ref[base + e]
        return total

    def copy(chain, step):
        return pltpu.make_async_remote_copy(
            src_ref=send[step].at[chain],
            dst_ref=recv[step].at[chain],
            send_sem=send_sem.at[chain, step],
            recv_sem=recv_sem.at[chain, step],
            device_id={"gx": partner(orders[chain][step])},
            device_id_type=MESH,
        )

    half = n // 2
    for chain in range(2):
        @pl.loop(0, half)
        def _(p):
            send[0][chain, p] = gathered(chain, half + p).astype(jnp.bfloat16)

        copy(chain, 0).start()
    for chain in range(2):
        @pl.loop(0, half)
        def _(p):
            acc[chain, p] = gathered(chain, p)

    for step in range(steps):
        count = half >> step
        for chain in range(2):
            copy(chain, step).wait_recv()
            if step + 1 < steps:
                keep = count // 2
                send[step + 1][chain] = (
                    acc[chain, keep:count] + recv[step][chain, keep:count].astype(jnp.float32)
                ).astype(jnp.bfloat16)
                copy(chain, step + 1).start()
                acc[chain, 0:keep] = acc[chain, 0:keep] + recv[step][chain, 0:keep].astype(
                    jnp.float32
                )
            else:
                out_ref[chain * rows : (chain + 1) * rows, :] = acc[chain, 0] + recv[step][
                    chain, 0
                ].astype(jnp.float32)
    for step in range(steps):
        for chain in range(2):
            copy(chain, step).wait_send()
    for i in range(4):
        @pl.when(sides[i][0])
        def _():
            halo(i).wait_send()


def body(blocks_a, prolong, aggregate, coupling_slot):
    grid_rows, grid_cols, block_len = prolong.shape
    elements = grid_rows * grid_cols
    n, ny = lax.axis_size("gx"), lax.axis_size("gy")
    matrix_a = blocks_a.reshape(elements * K, B, B)
    matrix_p = prolong.reshape(elements, B, B)

    orders = bit_orders(n)
    steps = len(orders[0])
    offsets = jnp.asarray([places(order) for order in orders], jnp.int32)
    owner_at = jnp.bitwise_xor(offsets, lax.axis_index("gx"))
    owners = aggregate.reshape(elements)
    owner_is = (owner_at[:, :, None] == owners[None, None, :]).astype(jnp.float32).reshape(-1)
    slots = coupling_slot.reshape(elements * K, 1)
    slot_is = (slots == jnp.arange(CS, dtype=jnp.int32)[None, :]).astype(jnp.float32).reshape(-1)

    places_of = [(2, n >> (step + 1), B // 2, CS * B) for step in range(steps)]
    vmem = pl.BlockSpec(memory_space=pltpu.VMEM)
    smem = pl.BlockSpec(memory_space=pltpu.SMEM)
    coarse = pl.pallas_call(
        functools.partial(coarsen, n, ny, orders),
        out_shape=jax.ShapeDtypeStruct((B, CS * B), jnp.float32),
        in_specs=[smem, smem, vmem, vmem],
        out_specs=vmem,
        scratch_shapes=[
            pltpu.VMEM((elements, B, B), jnp.bfloat16),
            pltpu.VMEM((elements, B, B), jnp.bfloat16),
            pltpu.VMEM((B, B), jnp.bfloat16),
            pltpu.VMEM((B, B), jnp.bfloat16),
            pltpu.VMEM((2, B, CS * B), jnp.bfloat16),
            pltpu.VMEM((elements, B, CS * B), jnp.float32),
            pltpu.VMEM(places_of[0], jnp.float32),
        ]
        + [pltpu.VMEM(shape, jnp.bfloat16) for shape in places_of + places_of]
        + [
            pltpu.SemaphoreType.DMA((2, steps)),
            pltpu.SemaphoreType.DMA((2, steps)),
            pltpu.SemaphoreType.DMA((4,)),
            pltpu.SemaphoreType.DMA((4,)),
        ],
        compiler_params=pltpu.CompilerParams(
            collective_id=0, has_side_effects=True, vmem_limit_bytes=40 * 1024 * 1024
        ),
    )(owner_is, slot_is, matrix_a, matrix_p)
    coarse = coarse.reshape(B, CS, B).transpose(1, 0, 2)
    return coarse.reshape(1, 1, CS, block_len)


def solution(mesh):
    return jax.shard_map(
        body,
        mesh=mesh,
        in_specs=(
            P("gx", "gy", None, None),
            P("gx", "gy", None),
            P("gx", "gy"),
            P("gx", "gy", None),
        ),
        out_specs=P("gx", "gy", None, None),
        check_vma=False,
    )
```

```python
import functools

import jax
import jax.numpy as jnp
from jax import lax
from jax.experimental import pallas as pl
from jax.experimental.pallas import tpu as pltpu
from jax.sharding import PartitionSpec as P

B = 64
K = 5
CS = 8
MESH = pl.DeviceIdType.MESH


def bit_orders(n):
    bits = [1 << i for i in range(n.bit_length() - 1)]
    first = min(3, len(bits))
    return [bits[i:first] + bits[:i] + bits[first:] for i in range(first)]


def places(order):
    offsets = [0]
    for bit in reversed(order):
        offsets = offsets + [o | bit for o in offsets]
    return offsets


def coarsen(
    n, ny, orders, owner_ref, slot_ref, a_ref, p_ref, out_ref,
    low_x, high_x, low_y, high_y, products, sums, parts, acc, *rest,
):
    steps = len(orders[0])
    send, recv = rest[:steps], rest[steps : 2 * steps]
    send_sem, recv_sem, halo_send, halo_recv = rest[2 * steps :]
    me, column = lax.axis_index("gx"), lax.axis_index("gy")
    elements = p_ref.shape[0]
    chains = send[0].shape[0]
    rows, width = send[0].shape[2:]
    bands = p_ref.shape[1] // rows

    def part_of(chain):
        low, left = (chain % bands) * rows, (chain // bands) * width
        return slice(low, low + rows), slice(left, left + width)

    def partner(bit):
        return me + bit - 2 * bit * ((me // bit) % 2)

    sides = [
        (me < n - 1, me > 0, {"gx": jnp.minimum(me + 1, n - 1)}, p_ref, low_x),
        (me > 0, me < n - 1, {"gx": jnp.maximum(me - 1, 0)}, p_ref, high_x),
        (column < ny - 1, column > 0, {"gy": jnp.minimum(column + 1, ny - 1)},
         p_ref.at[elements - 1], low_y),
        (column > 0, column < ny - 1, {"gy": jnp.maximum(column - 1, 0)}, p_ref.at[0], high_y),
    ]

    def halo(i):
        return pltpu.make_async_remote_copy(
            src_ref=sides[i][3], dst_ref=sides[i][4],
            send_sem=halo_send.at[i], recv_sem=halo_recv.at[i],
            device_id=sides[i][2], device_id_type=MESH,
        )

    barrier = pltpu.get_barrier_semaphore()
    for bit in orders[0]:
        pl.semaphore_signal(
            barrier, inc=1, device_id={"gx": partner(bit)}, device_id_type=MESH
        )
    for sends, _, target, _, _ in sides:
        @pl.when(sends)
        def _():
            pl.semaphore_signal(barrier, inc=1, device_id=target, device_id_type=MESH)
    expected = steps
    for sends, _, _, _, _ in sides:
        expected = expected + jnp.where(sends, 1, 0)
    pl.semaphore_wait(barrier, expected)
    for i, (sends, receives, _, _, place) in enumerate(sides):
        @pl.when(sends)
        def _():
            halo(i).start()

        @pl.when(jnp.logical_not(receives))
        def _():
            place[...] = jnp.zeros_like(place)

    def multiply(e, k, block):
        products[e * K + k] = jnp.dot(
            a_ref[e * K + k], block, preferred_element_type=jnp.float32
        ).astype(jnp.bfloat16)

    for e in range(elements):
        multiply(e, 0, p_ref[e])
        if e:
            multiply(e, 3, p_ref[e - 1])
        if e + 1 < elements:
            multiply(e, 4, p_ref[e + 1])
    for i in range(4):
        @pl.when(sides[i][1])
        def _():
            halo(i).wait_recv()
    multiply(0, 3, low_y[...])
    multiply(elements - 1, 4, high_y[...])

    for e in range(elements):
        multiply(e, 1, low_x[e])
        multiply(e, 2, high_x[e])
        terms = [products[e * K + k].astype(jnp.float32) for k in range(K)]
        for s in range(CS):
            total = terms[0] * jnp.where(slot_ref[e * K] == s, 1.0, 0.0)
            for k in range(1, K):
                total = total + terms[k] * jnp.where(slot_ref[e * K + k] == s, 1.0, 0.0)
            sums[e % 2, :, s * B : (s + 1) * B] = total.astype(jnp.bfloat16)
        parts[e] = (
            lax.dot_general(
                p_ref[e], sums[e % 2], (((0,), (0,)), ((), ())),
                preferred_element_type=jnp.float32,
            ).astype(jnp.bfloat16).astype(jnp.float32)
        )

    def gathered(chain, place):
        band, lanes = part_of(chain)
        base = (chain % len(orders) * n + place) * elements
        total = parts[0, band, lanes] * owner_ref[base]
        for e in range(1, elements):
            total = total + parts[e, band, lanes] * owner_ref[base + e]
        return total

    def copy(chain, step):
        return pltpu.make_async_remote_copy(
            src_ref=send[step].at[chain],
            dst_ref=recv[step].at[chain],
            send_sem=send_sem.at[chain, step],
            recv_sem=recv_sem.at[chain, step],
            device_id={"gx": partner(orders[chain % len(orders)][step])},
            device_id_type=MESH,
        )

    half = n // 2
    for chain in range(chains):
        @pl.loop(0, half)
        def _(p):
            send[0][chain, p] = gathered(chain, half + p).astype(jnp.bfloat16)

        copy(chain, 0).start()
    for chain in range(chains):
        @pl.loop(0, half)
        def _(p):
            acc[chain, p] = gathered(chain, p)

    for step in range(steps):
        count = half >> step
        for chain in range(chains):
            copy(chain, step).wait_recv()
            if step + 1 < steps:
                keep = count // 2
                send[step + 1][chain] = (
                    acc[chain, keep:count] + recv[step][chain, keep:count].astype(jnp.float32)
                ).astype(jnp.bfloat16)
                copy(chain, step + 1).start()
                acc[chain, 0:keep] = acc[chain, 0:keep] + recv[step][chain, 0:keep].astype(
                    jnp.float32
                )
            else:
                band, lanes = part_of(chain)
                out_ref[band, lanes] = acc[chain, 0] + recv[step][
                    chain, 0
                ].astype(jnp.float32)
    for step in range(steps):
        for chain in range(chains):
            copy(chain, step).wait_send()
    for i in range(4):
        @pl.when(sides[i][0])
        def _():
            halo(i).wait_send()


def body(blocks_a, prolong, aggregate, coupling_slot):
    grid_rows, grid_cols, block_len = prolong.shape
    elements = grid_rows * grid_cols
    n, ny = lax.axis_size("gx"), lax.axis_size("gy")
    matrix_a = blocks_a.reshape(elements * K, B, B)
    matrix_p = prolong.reshape(elements, B, B)

    orders = bit_orders(n)
    steps = len(orders[0])
    offsets = jnp.asarray([places(order) for order in orders], jnp.int32)
    owner_at = jnp.bitwise_xor(offsets, lax.axis_index("gx"))
    owners = aggregate.reshape(elements)
    owner_is = (owner_at[:, :, None] == owners[None, None, :]).astype(jnp.float32).reshape(-1)
    slots = coupling_slot.reshape(elements * K)

    chains = 8
    places_of = [(chains, n >> (step + 1), B // 4, CS * B // 2) for step in range(steps)]
    vmem = pl.BlockSpec(memory_space=pltpu.VMEM)
    smem = pl.BlockSpec(memory_space=pltpu.SMEM)
    coarse = pl.pallas_call(
        functools.partial(coarsen, n, ny, orders),
        out_shape=jax.ShapeDtypeStruct((B, CS * B), jnp.float32),
        in_specs=[smem, smem, vmem, vmem],
        out_specs=vmem,
        scratch_shapes=[
            pltpu.VMEM((elements, B, B), jnp.bfloat16),
            pltpu.VMEM((elements, B, B), jnp.bfloat16),
            pltpu.VMEM((B, B), jnp.bfloat16),
            pltpu.VMEM((B, B), jnp.bfloat16),
            pltpu.VMEM((elements * K, B, B), jnp.bfloat16),
            pltpu.VMEM((2, B, CS * B), jnp.bfloat16),
            pltpu.VMEM((elements, B, CS * B), jnp.float32),
            pltpu.VMEM(places_of[0], jnp.float32),
        ]
        + [pltpu.VMEM(shape, jnp.bfloat16) for shape in places_of + places_of]
        + [
            pltpu.SemaphoreType.DMA((chains, steps)),
            pltpu.SemaphoreType.DMA((chains, steps)),
            pltpu.SemaphoreType.DMA((4,)),
            pltpu.SemaphoreType.DMA((4,)),
        ],
        compiler_params=pltpu.CompilerParams(
            collective_id=0, has_side_effects=True, vmem_limit_bytes=40 * 1024 * 1024
        ),
    )(owner_is, slots, matrix_a, matrix_p)
    coarse = coarse.reshape(B, CS, B).transpose(1, 0, 2)
    return coarse.reshape(1, 1, CS, block_len)


def solution(mesh):
    return jax.shard_map(
        body,
        mesh=mesh,
        in_specs=(
            P("gx", "gy", None, None),
            P("gx", "gy", None),
            P("gx", "gy"),
            P("gx", "gy", None),
        ),
        out_specs=P("gx", "gy", None, None),
        check_vma=False,
    )
```

```python
import functools

import jax
import jax.numpy as jnp
from jax import lax
from jax.experimental import pallas as pl
from jax.experimental.pallas import tpu as pltpu
from jax.sharding import PartitionSpec as P

B = 64
K = 5
CS = 8
MESH = pl.DeviceIdType.MESH


def bit_orders(n):
    bits = [1 << i for i in range(n.bit_length() - 1)]
    first = min(3, len(bits))
    return [bits[i:first] + bits[:i] + bits[first:] for i in range(first)]


def places(orders, n):
    which = lax.broadcasted_iota(jnp.int32, (len(orders), n), 0)
    place = lax.broadcasted_iota(jnp.int32, (len(orders), n), 1)
    offsets = jnp.zeros_like(place)
    for i, order in enumerate(orders):
        for step, bit in enumerate(order):
            on = (place >> (len(order) - 1 - step)) & 1
            offsets = offsets + jnp.where(which == i, on * bit, 0)
    return offsets


def coarsen(
    n, ny, orders, owner_ref, slot_ref, a_ref, p_ref, out_ref,
    low_x, high_x, low_y, high_y, products, sums, parts, acc, *rest,
):
    steps = len(orders[0])
    send, recv = rest[:steps], rest[steps : 2 * steps]
    send_sem, recv_sem, halo_send, halo_recv = rest[2 * steps :]
    me, column = lax.axis_index("gx"), lax.axis_index("gy")
    elements = p_ref.shape[0]
    chains = send[0].shape[0]
    rows, width = send[0].shape[2:]
    bands = p_ref.shape[1] // rows

    def part_of(chain):
        low, left = (chain % bands) * rows, (chain // bands) * width
        return slice(low, low + rows), slice(left, left + width)

    def partner(bit):
        return me + bit - 2 * bit * ((me // bit) % 2)

    sides = [
        (me < n - 1, me > 0, {"gx": jnp.minimum(me + 1, n - 1)}, p_ref, low_x),
        (me > 0, me < n - 1, {"gx": jnp.maximum(me - 1, 0)}, p_ref, high_x),
        (column < ny - 1, column > 0, {"gy": jnp.minimum(column + 1, ny - 1)},
         p_ref.at[elements - 1], low_y),
        (column > 0, column < ny - 1, {"gy": jnp.maximum(column - 1, 0)}, p_ref.at[0], high_y),
    ]

    def halo(i):
        return pltpu.make_async_remote_copy(
            src_ref=sides[i][3], dst_ref=sides[i][4],
            send_sem=halo_send.at[i], recv_sem=halo_recv.at[i],
            device_id=sides[i][2], device_id_type=MESH,
        )

    barrier = pltpu.get_barrier_semaphore()
    for bit in orders[0]:
        pl.semaphore_signal(
            barrier, inc=1, device_id={"gx": partner(bit)}, device_id_type=MESH
        )
    for sends, _, target, _, _ in sides:
        @pl.when(sends)
        def _():
            pl.semaphore_signal(barrier, inc=1, device_id=target, device_id_type=MESH)
    expected = steps
    for sends, _, _, _, _ in sides:
        expected = expected + jnp.where(sends, 1, 0)
    pl.semaphore_wait(barrier, expected)
    for i, (sends, receives, _, _, place) in enumerate(sides):
        @pl.when(sends)
        def _():
            halo(i).start()

        @pl.when(jnp.logical_not(receives))
        def _():
            place[...] = jnp.zeros_like(place)

    def multiply(e, k, block):
        products[e * K + k] = jnp.dot(
            a_ref[k * elements + e], block, preferred_element_type=jnp.float32
        ).astype(jnp.bfloat16)

    for e in range(elements):
        multiply(e, 0, p_ref[e])
        if e:
            multiply(e, 3, p_ref[e - 1])
        if e + 1 < elements:
            multiply(e, 4, p_ref[e + 1])
    for i in range(4):
        @pl.when(sides[i][1])
        def _():
            halo(i).wait_recv()
    multiply(0, 3, low_y[...])
    multiply(elements - 1, 4, high_y[...])

    for e in range(elements):
        multiply(e, 1, low_x[e])
        multiply(e, 2, high_x[e])
        terms = [products[e * K + k].astype(jnp.float32) for k in range(K)]
        for s in range(CS):
            total = terms[0] * jnp.where(slot_ref[e] == s, 1.0, 0.0)
            for k in range(1, K):
                total = total + terms[k] * jnp.where(slot_ref[k * elements + e] == s, 1.0, 0.0)
            sums[e % 2, :, s * B : (s + 1) * B] = total.astype(jnp.bfloat16)
        parts[e] = (
            lax.dot_general(
                p_ref[e], sums[e % 2], (((0,), (0,)), ((), ())),
                preferred_element_type=jnp.float32,
            ).astype(jnp.bfloat16).astype(jnp.float32)
        )

    def gathered(chain, place):
        band, lanes = part_of(chain)
        base = (chain % len(orders) * n + place) * elements
        total = parts[0, band, lanes] * owner_ref[base]
        for e in range(1, elements):
            total = total + parts[e, band, lanes] * owner_ref[base + e]
        return total

    def copy(chain, step):
        return pltpu.make_async_remote_copy(
            src_ref=send[step].at[chain],
            dst_ref=recv[step].at[chain],
            send_sem=send_sem.at[chain, step],
            recv_sem=recv_sem.at[chain, step],
            device_id={"gx": partner(orders[chain % len(orders)][step])},
            device_id_type=MESH,
        )

    half = n // 2
    for chain in range(chains):
        @pl.loop(0, half, unroll=4)
        def _(p):
            send[0][chain, p] = gathered(chain, half + p).astype(jnp.bfloat16)

        copy(chain, 0).start()
    for chain in range(chains):
        @pl.loop(0, half, unroll=4)
        def _(p):
            acc[chain, p] = gathered(chain, p)

    for step in range(steps):
        count = half >> step
        for chain in range(chains):
            copy(chain, step).wait_recv()
            if step + 1 < steps:
                keep = count // 2
                send[step + 1][chain] = (
                    acc[chain, keep:count] + recv[step][chain, keep:count].astype(jnp.float32)
                ).astype(jnp.bfloat16)
                copy(chain, step + 1).start()
                acc[chain, 0:keep] = acc[chain, 0:keep] + recv[step][chain, 0:keep].astype(
                    jnp.float32
                )
            else:
                band, lanes = part_of(chain)
                out_ref[band, lanes] = acc[chain, 0] + recv[step][
                    chain, 0
                ].astype(jnp.float32)
    for step in range(steps):
        for chain in range(chains):
            copy(chain, step).wait_send()
    for i in range(4):
        @pl.when(sides[i][0])
        def _():
            halo(i).wait_send()


def body(blocks_a, prolong, aggregate, coupling_slot):
    grid_rows, grid_cols, block_len = prolong.shape
    elements = grid_rows * grid_cols
    n, ny = lax.axis_size("gx"), lax.axis_size("gy")
    matrix_a = blocks_a.transpose(2, 0, 1, 3).reshape(K * elements, B, B)
    matrix_p = prolong.reshape(elements, B, B)

    orders = bit_orders(n)
    steps = len(orders[0])
    offsets = places(orders, n)
    owner_at = jnp.bitwise_xor(offsets, lax.axis_index("gx"))
    owners = aggregate.reshape(elements)
    owner_is = (owner_at[:, :, None] == owners[None, None, :]).astype(jnp.float32).reshape(-1)
    slots = coupling_slot.transpose(2, 0, 1).reshape(K * elements)

    chains = 8
    places_of = [(chains, n >> (step + 1), B // 4, CS * B // 2) for step in range(steps)]
    vmem = pl.BlockSpec(memory_space=pltpu.VMEM)
    smem = pl.BlockSpec(memory_space=pltpu.SMEM)
    coarse = pl.pallas_call(
        functools.partial(coarsen, n, ny, orders),
        out_shape=jax.ShapeDtypeStruct((B, CS * B), jnp.float32),
        in_specs=[smem, smem, vmem, vmem],
        out_specs=vmem,
        scratch_shapes=[
            pltpu.VMEM((elements, B, B), jnp.bfloat16),
            pltpu.VMEM((elements, B, B), jnp.bfloat16),
            pltpu.VMEM((B, B), jnp.bfloat16),
            pltpu.VMEM((B, B), jnp.bfloat16),
            pltpu.VMEM((elements * K, B, B), jnp.bfloat16),
            pltpu.VMEM((2, B, CS * B), jnp.bfloat16),
            pltpu.VMEM((elements, B, CS * B), jnp.float32),
            pltpu.VMEM(places_of[0], jnp.float32),
        ]
        + [pltpu.VMEM(shape, jnp.bfloat16) for shape in places_of + places_of]
        + [
            pltpu.SemaphoreType.DMA((chains, steps)),
            pltpu.SemaphoreType.DMA((chains, steps)),
            pltpu.SemaphoreType.DMA((4,)),
            pltpu.SemaphoreType.DMA((4,)),
        ],
        compiler_params=pltpu.CompilerParams(
            collective_id=0, has_side_effects=True, vmem_limit_bytes=40 * 1024 * 1024
        ),
    )(owner_is, slots, matrix_a, matrix_p)
    coarse = coarse.reshape(B, CS, B).transpose(1, 0, 2)
    return coarse.reshape(1, 1, CS, block_len)


def solution(mesh):
    return jax.shard_map(
        body,
        mesh=mesh,
        in_specs=(
            P("gx", "gy", None, None),
            P("gx", "gy", None),
            P("gx", "gy"),
            P("gx", "gy", None),
        ),
        out_specs=P("gx", "gy", None, None),
        check_vma=False,
    )
```

```python
import functools

import jax
import jax.numpy as jnp
from jax import lax
from jax.experimental import pallas as pl
from jax.experimental.pallas import tpu as pltpu
from jax.sharding import PartitionSpec as P

B = 64
K = 5
CS = 8
MESH = pl.DeviceIdType.MESH


def bit_orders(n):
    bits = [1 << i for i in range(n.bit_length() - 1)]
    first = min(3, len(bits))
    return [bits[i:first] + bits[:i] + bits[first:] for i in range(first)]


def places(orders, n):
    which = lax.broadcasted_iota(jnp.int32, (len(orders), n), 0)
    place = lax.broadcasted_iota(jnp.int32, (len(orders), n), 1)
    offsets = jnp.zeros_like(place)
    for i, order in enumerate(orders):
        for step, bit in enumerate(order):
            on = (place >> (len(order) - 1 - step)) & 1
            offsets = offsets + jnp.where(which == i, on * bit, 0)
    return offsets


def coarsen(
    n, ny, orders, owner_ref, slot_ref, a_ref, p_ref, out_ref,
    low_x, high_x, low_y, high_y, products, sums, parts, acc, *rest,
):
    steps = len(orders[0])
    send, recv = rest[:steps], rest[steps : 2 * steps]
    send_sem, recv_sem, halo_send, halo_recv = rest[2 * steps :]
    me, column = lax.axis_index("gx"), lax.axis_index("gy")
    elements = p_ref.shape[0]
    chains = send[0].shape[0]
    rows, width = send[0].shape[2:]
    bands = p_ref.shape[1] // rows

    def part_of(chain):
        low, left = (chain % bands) * rows, (chain // bands) * width
        return slice(low, low + rows), slice(left, left + width)

    def partner(bit):
        return me + bit - 2 * bit * ((me // bit) % 2)

    sides = [
        (me < n - 1, me > 0, {"gx": jnp.minimum(me + 1, n - 1)}, p_ref, low_x),
        (me > 0, me < n - 1, {"gx": jnp.maximum(me - 1, 0)}, p_ref, high_x),
        (column < ny - 1, column > 0, {"gy": jnp.minimum(column + 1, ny - 1)},
         p_ref.at[elements - 1], low_y),
        (column > 0, column < ny - 1, {"gy": jnp.maximum(column - 1, 0)}, p_ref.at[0], high_y),
    ]

    def halo(i):
        return pltpu.make_async_remote_copy(
            src_ref=sides[i][3], dst_ref=sides[i][4],
            send_sem=halo_send.at[i], recv_sem=halo_recv.at[i],
            device_id=sides[i][2], device_id_type=MESH,
        )

    barrier = pltpu.get_barrier_semaphore()
    for bit in orders[0]:
        pl.semaphore_signal(
            barrier, inc=1, device_id={"gx": partner(bit)}, device_id_type=MESH
        )
    for sends, _, target, _, _ in sides:
        @pl.when(sends)
        def _():
            pl.semaphore_signal(barrier, inc=1, device_id=target, device_id_type=MESH)
    expected = steps
    for sends, _, _, _, _ in sides:
        expected = expected + jnp.where(sends, 1, 0)
    pl.semaphore_wait(barrier, expected)
    for i, (sends, receives, _, _, place) in enumerate(sides):
        @pl.when(sends)
        def _():
            halo(i).start()

        @pl.when(jnp.logical_not(receives))
        def _():
            place[...] = jnp.zeros_like(place)

    def multiply(e, k, block):
        products[e * K + k] = jnp.dot(
            a_ref[k * elements + e], block, preferred_element_type=jnp.float32
        ).astype(jnp.bfloat16)

    for e in range(elements):
        multiply(e, 0, p_ref[e])
        if e:
            multiply(e, 3, p_ref[e - 1])
        if e + 1 < elements:
            multiply(e, 4, p_ref[e + 1])
    for i in range(4):
        @pl.when(sides[i][1])
        def _():
            halo(i).wait_recv()
    multiply(0, 3, low_y[...])
    multiply(elements - 1, 4, high_y[...])

    for e in range(elements):
        multiply(e, 1, low_x[e])
        multiply(e, 2, high_x[e])
        terms = [products[e * K + k].astype(jnp.float32) for k in range(K)]
        for s in range(CS):
            total = terms[0] * jnp.where(slot_ref[e] == s, 1.0, 0.0)
            for k in range(1, K):
                total = total + terms[k] * jnp.where(slot_ref[k * elements + e] == s, 1.0, 0.0)
            sums[e % 2, :, s * B : (s + 1) * B] = total.astype(jnp.bfloat16)
        parts[e] = (
            lax.dot_general(
                p_ref[e], sums[e % 2], (((0,), (0,)), ((), ())),
                preferred_element_type=jnp.float32,
            ).astype(jnp.bfloat16).astype(jnp.float32)
        )

    def gathered(chain, place):
        band, lanes = part_of(chain)
        base = (chain % len(orders) * n + place) * elements
        total = parts[0, band, lanes] * owner_ref[base]
        for e in range(1, elements):
            total = total + parts[e, band, lanes] * owner_ref[base + e]
        return total

    def copy(chain, step):
        return pltpu.make_async_remote_copy(
            src_ref=send[step].at[chain],
            dst_ref=recv[step].at[chain],
            send_sem=send_sem.at[chain, step],
            recv_sem=recv_sem.at[chain, step],
            device_id={"gx": partner(orders[chain % len(orders)][step])},
            device_id_type=MESH,
        )

    half = n // 2
    for chain in range(chains):
        @pl.loop(0, half, unroll=4)
        def _(p):
            send[0][chain, p] = gathered(chain, half + p).astype(jnp.bfloat16)

        copy(chain, 0).start()
    for chain in range(chains):
        @pl.loop(0, half, unroll=4)
        def _(p):
            acc[chain, p] = gathered(chain, p)

    for step in range(steps):
        count = half >> step
        for chain in range(chains):
            copy(chain, step).wait_recv()
            if step + 1 < steps:
                keep = count // 2
                send[step + 1][chain] = (
                    acc[chain, keep:count] + recv[step][chain, keep:count].astype(jnp.float32)
                ).astype(jnp.bfloat16)
                copy(chain, step + 1).start()
            else:
                band, lanes = part_of(chain)
                out_ref[band, lanes] = acc[chain, 0] + recv[step][
                    chain, 0
                ].astype(jnp.float32)
        if step + 1 < steps:
            keep = count // 2
            for chain in range(chains):
                acc[chain, 0:keep] = acc[chain, 0:keep] + recv[step][chain, 0:keep].astype(
                    jnp.float32
                )
    for step in range(steps):
        for chain in range(chains):
            copy(chain, step).wait_send()
    for i in range(4):
        @pl.when(sides[i][0])
        def _():
            halo(i).wait_send()


def body(blocks_a, prolong, aggregate, coupling_slot):
    grid_rows, grid_cols, block_len = prolong.shape
    elements = grid_rows * grid_cols
    n, ny = lax.axis_size("gx"), lax.axis_size("gy")
    matrix_a = blocks_a.transpose(2, 0, 1, 3).reshape(K * elements, B, B)
    matrix_p = prolong.reshape(elements, B, B)

    orders = bit_orders(n)
    steps = len(orders[0])
    offsets = places(orders, n)
    owner_at = jnp.bitwise_xor(offsets, lax.axis_index("gx"))
    owners = aggregate.reshape(elements)
    owner_is = (owner_at[:, :, None] == owners[None, None, :]).astype(jnp.float32).reshape(-1)
    slots = coupling_slot.transpose(2, 0, 1).reshape(K * elements)

    chains = 8
    places_of = [(chains, n >> (step + 1), B // 4, CS * B // 2) for step in range(steps)]
    vmem = pl.BlockSpec(memory_space=pltpu.VMEM)
    smem = pl.BlockSpec(memory_space=pltpu.SMEM)
    coarse = pl.pallas_call(
        functools.partial(coarsen, n, ny, orders),
        out_shape=jax.ShapeDtypeStruct((B, CS * B), jnp.float32),
        in_specs=[smem, smem, vmem, vmem],
        out_specs=vmem,
        scratch_shapes=[
            pltpu.VMEM((elements, B, B), jnp.bfloat16),
            pltpu.VMEM((elements, B, B), jnp.bfloat16),
            pltpu.VMEM((B, B), jnp.bfloat16),
            pltpu.VMEM((B, B), jnp.bfloat16),
            pltpu.VMEM((elements * K, B, B), jnp.bfloat16),
            pltpu.VMEM((2, B, CS * B), jnp.bfloat16),
            pltpu.VMEM((elements, B, CS * B), jnp.float32),
            pltpu.VMEM(places_of[0], jnp.float32),
        ]
        + [pltpu.VMEM(shape, jnp.bfloat16) for shape in places_of + places_of]
        + [
            pltpu.SemaphoreType.DMA((chains, steps)),
            pltpu.SemaphoreType.DMA((chains, steps)),
            pltpu.SemaphoreType.DMA((4,)),
            pltpu.SemaphoreType.DMA((4,)),
        ],
        compiler_params=pltpu.CompilerParams(
            collective_id=0, has_side_effects=True, vmem_limit_bytes=40 * 1024 * 1024
        ),
    )(owner_is, slots, matrix_a, matrix_p)
    coarse = coarse.reshape(B, CS, B).transpose(1, 0, 2)
    return coarse.reshape(1, 1, CS, block_len)


def solution(mesh):
    return jax.shard_map(
        body,
        mesh=mesh,
        in_specs=(
            P("gx", "gy", None, None),
            P("gx", "gy", None),
            P("gx", "gy"),
            P("gx", "gy", None),
        ),
        out_specs=P("gx", "gy", None, None),
        check_vma=False,
    )
```
